512 devices in a mesh: row: 16 (over z_hi, y), col: 32 (over z_lo, x, core).
Axes of the slice: x: 4, y: 4, z: 16 (z_hi: 4, z_lo: 4; z = z_hi * 4 + z_lo), core: 2. Of those that a mesh axis runs over, the one named last changes fastest.
Arguments:
- inverse_block: bfloat16 [6144, 6144], P('row', 'col')
- panels: bfloat16 [2, 6144, 4096], P(None, 'row', 'col'), may hold values from -0.078125 to 0.078125
- structure: int32 [2, 48], replicated, may hold values 0 or 1
- pivot_inverse: bfloat16 [2, 4096, 4096], P(None, 'row', 'col')
Outputs:
- panel_inverse: bfloat16 [2, 6144, 4096], P(None, 'row', 'col')
- diagonal_inverse: bfloat16 [2, 4096, 4096], P(None, 'row', 'col')
The draws below stay inside these ranges and needn't reach their ends.
All inputs are finite; a program needn't handle non-finite values.
Results may differ from the reference program's by a relative error of at most 0.019.
Values may be sent and summed in bfloat16 or wider, within the bound.
No kernel may reach another device: no remote copies, remote signals or barrier semaphores. Data moves between devices by JAX's collectives and lax.ppermute only.
A program may use at most 64 MiB of HBM per device.

```python
import jax
import jax.numpy as jnp

WIDTH = 4096
SUPERNODES = 2
TILE = 128
ROWS_DEV = 384
ANCESTORS = 6144
N_ROW = 16


def draw_inverse_block(key, part):
    key = jax.random.fold_in(key, 3)
    normal_part = jax.random.normal(key, (ANCESTORS, ANCESTORS), jnp.float32)
    symmetric = (normal_part + normal_part.T) * 0.7071 + 2.0 * jnp.eye(ANCESTORS, dtype=jnp.float32)
    return symmetric.astype(jnp.bfloat16)


def draw_pivot_inverse(key, part):
    key = jax.random.fold_in(key, 11)
    normal_part = jax.random.normal(key, (SUPERNODES, WIDTH, WIDTH), jnp.float32)
    symmetric = (normal_part + jnp.swapaxes(normal_part, 1, 2)) * 0.35
    return (symmetric + jnp.eye(WIDTH, dtype=jnp.float32)[None, :, :]).astype(jnp.bfloat16)


def set_ends(values, stream_key, least, largest):
    place = [jax.random.randint(jax.random.fold_in(stream_key, axis), (), 0, length) for axis, length in enumerate(values.shape)]
    widest = values.shape.index(max(values.shape))
    beside = place[:widest] + [(place[widest] + 1) % values.shape[widest]] + place[widest + 1:]
    return values.at[tuple(place)].set(least).at[tuple(beside)].set(largest)


def shard_levels(stream_key, dims, shards, low, largest):
    def one(axis_at, blocks):
        draws = jax.random.uniform(jax.random.fold_in(jax.random.fold_in(stream_key, 6), axis_at), (blocks,), jnp.float32, low / len(shards), largest / len(shards))
        return jnp.repeat(jnp.exp(draws), dims[axis_at] // blocks).reshape((-1,) + (1,) * (len(dims) - axis_at - 1))

    level = one(*shards[0])
    for cut in shards[1:]:
        level = level * one(*cut)
    return level


def scatter_about(stream_key, dims, width, reach, shards=(), held_as=jnp.bfloat16):
    gain = shard_levels(stream_key, dims, shards, -0.22, 0.18) if shards else 1.0
    array = jax.random.normal(stream_key, dims, jnp.float32) * width * gain
    return jnp.minimum(jnp.maximum(array, -reach), reach).astype(held_as)


def setup_inputs(seed: int = 0) -> dict:
    key_list = jax.random.split(jax.random.key(seed), 5)
    return {
        "inverse_block": draw_inverse_block(jax.random.fold_in(key_list[4], 71), 0),
        "panels": scatter_about(key_list[1], (SUPERNODES, ANCESTORS, WIDTH), ANCESTORS ** -0.5, 0.078125, ((1, 16), (2, 32))),
        "structure": set_ends((jax.random.randint(key_list[2], (SUPERNODES, ANCESTORS // TILE), 0, 4) < 3).astype(jnp.int32), jax.random.fold_in(key_list[2], 1), 0, 1),
        "pivot_inverse": draw_pivot_inverse(jax.random.fold_in(key_list[4], 71), 0),
    }


def reference(inverse_block, panels, structure, pivot_inverse):
    flags = jnp.repeat(structure, TILE, axis=1).astype(jnp.bfloat16)
    masked = panels * flags[:, :, None]
    panel_list = []
    diagonal_list = []
    for sup in range(SUPERNODES):
        product = jnp.dot(inverse_block, masked[sup], preferred_element_type=jnp.float32)
        row_weight = flags[sup].astype(jnp.float32)[:, None]
        panel_part = (-(product * row_weight)).astype(jnp.bfloat16)
        left_groups = masked[sup].reshape(N_ROW, ROWS_DEV, WIDTH).astype(jnp.float32)
        right_groups = panel_part.reshape(N_ROW, ROWS_DEV, WIDTH).astype(jnp.float32)
        partial_value = jnp.einsum("gsi,gsj->gij", left_groups, right_groups).astype(jnp.bfloat16)
        summed = jnp.sum(partial_value.astype(jnp.float32), axis=0)
        diagonal_part = (pivot_inverse[sup].astype(jnp.float32) - summed).astype(jnp.bfloat16)
        panel_list.append(panel_part)
        diagonal_list.append(diagonal_part)
    return jnp.stack(panel_list), jnp.stack(diagonal_list)
```

```python
import functools

import jax
import jax.numpy as jnp
from jax import lax
from jax.experimental import pallas as pl
from jax.experimental.pallas import tpu as pltpu
from jax.sharding import Mesh, PartitionSpec as P

SUPERNODES = 2
TILE = 128
AXES = ("zh", "y", "zl", "x", "core")
SIZES = (4, 4, 4, 4, 2)
CONTRACT_ROWS = (((0,), (0,)), ((), ()))


def device_index(zh, y, zl, x, core):
    return (((zh * 4 + y) * 4 + zl) * 4 + x) * 2 + core


def transpose_pairs():
    pairs = []
    for zh in range(4):
        for y in range(4):
            for zl in range(4):
                for x in range(4):
                    for core in range(2):
                        pairs.append((device_index(zh, y, zl, x, core), device_index(zh, x, zl, y, core)))
    return pairs


def panel_kernel(block_ref, rows_ref, weight_ref, out_ref, acc_ref):
    step = pl.program_id(0)

    @pl.when(step == 0)
    def _():
        acc_ref[...] = jnp.zeros_like(acc_ref)

    acc_ref[...] += lax.dot_general(
        block_ref[...], rows_ref[0, 0], CONTRACT_ROWS, preferred_element_type=jnp.float32
    )

    @pl.when(step == pl.num_programs(0) - 1)
    def _():
        out_ref[...] = (-(acc_ref[...] * weight_ref[...])).astype(out_ref.dtype)


def panel_product(block_t, rows, weight):
    depth, width = rows.shape[2:]
    out_rows = block_t.shape[1]
    return pl.pallas_call(
        panel_kernel,
        grid=(16,),
        in_specs=[
            pl.BlockSpec((depth, out_rows), lambda s: (s, 0)),
            pl.BlockSpec((1, 1, depth, width), lambda s: (s % 4, s // 4, 0, 0)),
            pl.BlockSpec((out_rows, width), lambda s: (0, 0)),
        ],
        out_specs=pl.BlockSpec((out_rows, width), lambda s: (0, 0)),
        out_shape=jax.ShapeDtypeStruct((out_rows, width), jnp.bfloat16),
        scratch_shapes=[pltpu.VMEM((out_rows, width), jnp.float32)],
        compiler_params=pltpu.CompilerParams(vmem_limit_bytes=32 * 1024 * 1024),
        cost_estimate=pl.CostEstimate(
            flops=2 * 16 * depth * out_rows * width, bytes_accessed=9 * 1024 * 1024, transcendentals=0
        ),
    )(block_t, rows, weight)


def diagonal_kernel(left_ref, right_ref, out_ref):
    for sup in range(SUPERNODES):
        cols = slice(sup * 128, sup * 128 + 128)
        total = jnp.zeros((128, 128), jnp.float32)
        for y in range(4):
            total += lax.dot_general(
                left_ref[0, y, 0, :, cols], right_ref[y, :, cols], CONTRACT_ROWS,
                preferred_element_type=jnp.float32,
            )
        out_ref[0, sup] = total.astype(out_ref.dtype)


def diagonal_partial(left, right):
    depth, width = right.shape[1:]
    return pl.pallas_call(
        diagonal_kernel,
        grid=(4, 2),
        in_specs=[
            pl.BlockSpec((1, 4, 1, depth, width), lambda a, c: (a, 0, c, 0, 0)),
            pl.BlockSpec((4, depth, width), lambda a, c: (0, 0, 0)),
        ],
        out_specs=pl.BlockSpec((1, SUPERNODES, 128, 128), lambda a, c: (a, 0, c, 0)),
        out_shape=jax.ShapeDtypeStruct((4, SUPERNODES, 256, 128), jnp.bfloat16),
        compiler_params=pltpu.CompilerParams(vmem_limit_bytes=32 * 1024 * 1024),
        cost_estimate=pl.CostEstimate(
            flops=2 * 1024 * 1536 * 256, bytes_accessed=8 * 1024 * 1024, transcendentals=0
        ),
    )(left, right)


def on_device(inverse_block, panels, structure, pivot_inverse):
    row_index = lax.axis_index("zh") * 4 + lax.axis_index("y")
    local_rows = panels.shape[1]
    tiles_here = local_rows // TILE
    tile_flags = lax.dynamic_slice_in_dim(structure, row_index * tiles_here, tiles_here, 1)
    row_flags = jnp.repeat(tile_flags, TILE, axis=1).astype(jnp.bfloat16)
    masked = panels * row_flags[:, :, None]
    wide = jnp.concatenate([masked[0], masked[1]], axis=1)
    weight = jnp.repeat(row_flags.astype(jnp.float32).T, 128, axis=1)

    block_t = lax.all_gather(inverse_block.T, ("zl", "x", "core"), axis=0, tiled=True)
    swapped = lax.ppermute(wide, AXES, transpose_pairs())
    columns = lax.all_gather(swapped, ("zl", "x", "core"), axis=0)
    columns = columns.reshape(4, 4, 2, local_rows, 256)

    rows = lax.all_gather(lax.all_gather(wide, "zh"), "y")
    panel = panel_product(block_t, rows, weight)
    panel_rows = lax.all_gather(panel, "y")
    partial = diagonal_partial(columns, panel_rows)
    shares = lax.all_to_all(partial, "zh", split_axis=0, concat_axis=0, tiled=True)
    summed = jnp.sum(shares.astype(jnp.float32), axis=0)
    diagonal_inverse = (pivot_inverse.astype(jnp.float32) - summed).astype(jnp.bfloat16)
    panel_inverse = jnp.stack([panel[:, :128], panel[:, 128:]])
    return (panel_inverse, diagonal_inverse)


def solution(mesh):
    fine = Mesh(mesh.devices.reshape(SIZES), AXES)
    row, col = ("zh", "y"), ("zl", "x", "core")
    in_specs = (P(row, col), P(None, row, col), P(), P(None, row, col))
    out_specs = (P(None, row, col), P(None, row, col))
    return jax.shard_map(
        on_device, mesh=fine, in_specs=in_specs, out_specs=out_specs, check_vma=False
    )
```

```python
import jax
import jax.numpy as jnp
from jax import lax
from jax.experimental import pallas as pl
from jax.experimental.pallas import tpu as pltpu
from jax.sharding import Mesh, PartitionSpec as P

SUPERNODES = 2
TILE = 128
AXES = ("zh", "y", "zl", "x", "core")
SIZES = (4, 4, 4, 4, 2)
CONTRACT_ROWS = (((0,), (0,)), ((), ()))
VMEM_BYTES = 40 * 1024 * 1024


def pairs(move):
    listed = []
    for zh in range(4):
        for y in range(4):
            for zl in range(4):
                for x in range(4):
                    for core in range(2):
                        place = []
                        for at in ((zh, y, zl, x, core), move(zh, y, zl, x, core)):
                            index = 0
                            for size, coordinate in zip(SIZES, at):
                                index = index * size + coordinate
                            place.append(index)
                        listed.append(tuple(place))
    return listed


SWAP_CORES = pairs(lambda zh, y, zl, x, core: (zh, y, zl, x, 1 - core))
TURN = pairs(lambda zh, y, zl, x, core: (zh, x, zl, y, core))


def move(value, listed):
    return lax.ppermute(value, AXES, listed)


def panel_kernel(core_ref, own_ref, other_ref, rows_ref, out_ref):
    half = own_ref.shape[2]
    core = core_ref[0]
    total = jnp.zeros(out_ref.shape[1:], jnp.float32)
    for group in range(4):
        for block, part in ((own_ref, core), (other_ref, 1 - core)):
            start = pl.multiple_of(part * half, half)
            total += lax.dot_general(
                block[0, group], rows_ref[group, pl.ds(start, half), :], CONTRACT_ROWS,
                preferred_element_type=jnp.float32,
            )
    out_ref[0] = total.astype(out_ref.dtype)


def panel_partial(core, own, other, rows):
    groups, steps, half, height = own.shape
    width = rows.shape[2]
    block = pl.BlockSpec((1, steps, half, height), lambda g, core: (g, 0, 0, 0))
    return pl.pallas_call(
        panel_kernel,
        grid_spec=pltpu.PrefetchScalarGridSpec(
            num_scalar_prefetch=1,
            grid=(groups,),
            in_specs=[block, block, pl.BlockSpec(rows.shape, lambda g, core: (0, 0, 0))],
            out_specs=pl.BlockSpec((1, height, width), lambda g, core: (g, 0, 0)),
        ),
        out_shape=jax.ShapeDtypeStruct((groups, height, width), jnp.bfloat16),
        compiler_params=pltpu.CompilerParams(vmem_limit_bytes=VMEM_BYTES),
        cost_estimate=pl.CostEstimate(
            flops=4 * groups * steps * half * height * width,
            bytes_accessed=7 * 1024 * 1024,
            transcendentals=0,
        ),
    )(core, own, other, rows)


def diagonal_kernel(left_ref, right_ref, out_ref):
    total = jnp.zeros((left_ref.shape[3], right_ref.shape[2]), jnp.float32)
    for y in range(4):
        total += lax.dot_general(
            left_ref[y, 0], right_ref[y], CONTRACT_ROWS, preferred_element_type=jnp.float32
        )
    value = total.astype(out_ref.dtype)
    out_ref[0, 0] = value[:, :128]
    out_ref[0, 1] = value[:, 128:]


def diagonal_partial(left, right):
    groups, steps, depth, width = left.shape
    return pl.pallas_call(
        diagonal_kernel,
        grid=(steps,),
        in_specs=[
            pl.BlockSpec((groups, 1, depth, width), lambda g: (0, g, 0, 0)),
            pl.BlockSpec(right.shape, lambda g: (0, 0, 0)),
        ],
        out_specs=pl.BlockSpec((1, 2, width, 128), lambda g: (g, 0, 0, 0)),
        out_shape=jax.ShapeDtypeStruct((4, 2, width, 128), jnp.bfloat16),
        compiler_params=pltpu.CompilerParams(vmem_limit_bytes=VMEM_BYTES),
        cost_estimate=pl.CostEstimate(
            flops=2 * groups * steps * depth * width * 256,
            bytes_accessed=5 * 1024 * 1024,
            transcendentals=0,
        ),
    )(left, right)


def on_device(inverse_block, panels, structure, pivot_inverse):
    core = lax.axis_index("core")
    first = core == 0
    row_index = lax.axis_index("zh") * 4 + lax.axis_index("y")
    local_rows = panels.shape[1]
    tiles_here = local_rows // TILE
    tile_flags = lax.dynamic_slice_in_dim(structure, row_index * tiles_here, tiles_here, 1)
    row_flags = jnp.repeat(tile_flags, TILE, axis=1).astype(jnp.bfloat16)
    masked = panels * row_flags[:, :, None]
    weight = jnp.where(first, row_flags[0], row_flags[1]).astype(jnp.float32)[:, None]

    def swap_halves(mine, theirs):
        got = move(theirs, SWAP_CORES)
        return jnp.where(first, mine, got), jnp.where(first, got, mine)

    wide = jnp.concatenate(
        swap_halves(jnp.where(first, masked[0], masked[1]), jnp.where(first, masked[1], masked[0])), axis=1
    )
    turned_block = move(inverse_block.T, TURN)
    turned_panel = move(wide, TURN)
    block_parts = lax.all_gather(turned_block, "zl")
    own = lax.all_gather(block_parts, "x")
    turned_panel, block_parts = lax.optimization_barrier((turned_panel, block_parts))
    panel_parts = lax.all_gather(turned_panel, "zl")
    columns = lax.all_gather(panel_parts, "x")
    wide, panel_parts = lax.optimization_barrier((wide, panel_parts))
    rows = lax.all_gather(wide, "zh")
    own, rows = lax.optimization_barrier((own, rows))
    other = move(own, SWAP_CORES)

    partial = panel_partial(jnp.reshape(core, (1,)).astype(jnp.int32), own, other, rows)
    parts = lax.all_to_all(partial, "y", split_axis=0, concat_axis=0, tiled=True)
    panel = (-(jnp.sum(parts.astype(jnp.float32), axis=0) * weight)).astype(jnp.bfloat16)
    panel_rows = lax.all_gather(panel, "y")
    left, right = panel[:, :128], panel[:, 128:]
    panel_inverse = jnp.stack(
        swap_halves(jnp.where(first, left, right), jnp.where(first, right, left))
    )

    shares = diagonal_partial(columns, panel_rows).reshape(8, 256, 128)
    shares = lax.all_to_all(shares, ("zh", "core"), split_axis=0, concat_axis=0, tiled=True)
    summed = jnp.sum(shares.reshape(4, 2, 256, 128).astype(jnp.float32), axis=0)
    diagonal_inverse = (pivot_inverse.astype(jnp.float32) - summed).astype(jnp.bfloat16)
    return (panel_inverse, diagonal_inverse)


def solution(mesh):
    fine = Mesh(mesh.devices.reshape(SIZES), AXES)
    row, col = ("zh", "y"), ("zl", "x", "core")
    in_specs = (P(row, col), P(None, row, col), P(), P(None, row, col))
    out_specs = (P(None, row, col), P(None, row, col))
    return jax.shard_map(
        on_device, mesh=fine, in_specs=in_specs, out_specs=out_specs, check_vma=False
    )
```

```python
import jax
import jax.numpy as jnp
from jax import lax
from jax.experimental import pallas as pl
from jax.experimental.pallas import tpu as pltpu
from jax.sharding import Mesh, PartitionSpec as P

SUPERNODES = 2
TILE = 128
AXES = ("zh", "y", "zl", "x", "core")
SIZES = (4, 4, 4, 4, 2)
CONTRACT_ROWS = (((0,), (0,)), ((), ()))
VMEM_BYTES = 60 * 1024 * 1024


def pairs(move):
    listed = []
    for zh in range(4):
        for y in range(4):
            for zl in range(4):
                for x in range(4):
                    for core in range(2):
                        place = []
                        for at in ((zh, y, zl, x, core), move(zh, y, zl, x, core)):
                            index = 0
                            for size, coordinate in zip(SIZES, at):
                                index = index * size + coordinate
                            place.append(index)
                        listed.append(tuple(place))
    return listed


SWAP_CORES = pairs(lambda zh, y, zl, x, core: (zh, y, zl, x, 1 - core))
TURN = pairs(lambda zh, y, zl, x, core: (zh, x, zl, y, core))


def move(value, listed):
    return lax.ppermute(value, AXES, listed)


def panel_kernel(block_ref, rows_ref, out_ref):
    half = block_ref.shape[3]
    total = jnp.zeros(out_ref.shape[1:], jnp.float32)
    for group in range(4):
        for part in range(2):
            total += lax.dot_general(
                block_ref[0, part, group], rows_ref[group, part * half : part * half + half, :],
                CONTRACT_ROWS, preferred_element_type=jnp.float32,
            )
    out_ref[0] = total.astype(out_ref.dtype)


def panel_partial(block, rows):
    groups, parts, steps, half, height = block.shape
    width = rows.shape[2]
    return pl.pallas_call(
        panel_kernel,
        grid=(groups,),
        in_specs=[
            pl.BlockSpec((1, parts, steps, half, height), lambda g: (g, 0, 0, 0, 0)),
            pl.BlockSpec(rows.shape, lambda g: (0, 0, 0)),
        ],
        out_specs=pl.BlockSpec((1, height, width), lambda g: (g, 0, 0)),
        out_shape=jax.ShapeDtypeStruct((groups, height, width), jnp.bfloat16),
        compiler_params=pltpu.CompilerParams(vmem_limit_bytes=VMEM_BYTES),
        cost_estimate=pl.CostEstimate(
            flops=4 * groups * steps * half * height * width,
            bytes_accessed=7 * 1024 * 1024,
            transcendentals=0,
        ),
    )(block, rows)


def diagonal_kernel(left_ref, right_ref, out_ref):
    total = jnp.zeros((left_ref.shape[3], right_ref.shape[2]), jnp.float32)
    for y in range(4):
        total += lax.dot_general(
            left_ref[y, 0], right_ref[y], CONTRACT_ROWS, preferred_element_type=jnp.float32
        )
    value = total.astype(out_ref.dtype)
    out_ref[0, 0] = value[:, :128]
    out_ref[0, 1] = value[:, 128:]


def diagonal_partial(left, right):
    groups, steps, depth, width = left.shape
    return pl.pallas_call(
        diagonal_kernel,
        grid=(steps,),
        in_specs=[
            pl.BlockSpec((groups, 1, depth, width), lambda g: (0, g, 0, 0)),
            pl.BlockSpec(right.shape, lambda g: (0, 0, 0)),
        ],
        out_specs=pl.BlockSpec((1, 2, width, 128), lambda g: (g, 0, 0, 0)),
        out_shape=jax.ShapeDtypeStruct((4, 2, width, 128), jnp.bfloat16),
        compiler_params=pltpu.CompilerParams(vmem_limit_bytes=VMEM_BYTES),
        cost_estimate=pl.CostEstimate(
            flops=2 * groups * steps * depth * width * 256,
            bytes_accessed=5 * 1024 * 1024,
            transcendentals=0,
        ),
    )(left, right)


def on_device(inverse_block, panels, structure, pivot_inverse):
    core = lax.axis_index("core")
    first = core == 0
    row_index = lax.axis_index("zh") * 4 + lax.axis_index("y")
    local_rows = panels.shape[1]
    tiles_here = local_rows // TILE
    tile_flags = lax.dynamic_slice_in_dim(structure, row_index * tiles_here, tiles_here, 1)
    row_flags = jnp.repeat(tile_flags, TILE, axis=1).astype(jnp.bfloat16)
    masked = panels * row_flags[:, :, None]
    weight = jnp.where(first, row_flags[0], row_flags[1]).astype(jnp.float32)[:, None]

    def swap_halves(mine, theirs):
        got = move(theirs, SWAP_CORES)
        return jnp.where(first, mine, got), jnp.where(first, got, mine)

    wide = jnp.concatenate(
        swap_halves(jnp.where(first, masked[0], masked[1]), jnp.where(first, masked[1], masked[0])), axis=1
    )
    turned_block = move(inverse_block.T, TURN)
    turned_block, wide = lax.optimization_barrier((turned_block, wide))
    turned_panel = move(wide, TURN)
    block_parts = lax.all_gather(turned_block, "zl")
    block = lax.all_gather(block_parts, ("x", "core")).reshape((4, 2) + block_parts.shape)
    turned_panel, block_parts = lax.optimization_barrier((turned_panel, block_parts))
    panel_parts = lax.all_gather(turned_panel, "zl")
    columns = lax.all_gather(panel_parts, "x")
    wide, panel_parts = lax.optimization_barrier((wide, panel_parts))
    rows = lax.all_gather(wide, "zh")
    block, rows = lax.optimization_barrier((block, rows))
    partial = panel_partial(block, rows)
    parts = lax.all_to_all(partial, "y", split_axis=0, concat_axis=0, tiled=True)
    panel = (-(jnp.sum(parts.astype(jnp.float32), axis=0) * weight)).astype(jnp.bfloat16)
    panel_rows = lax.all_gather(panel, "y")
    left, right = panel[:, :128], panel[:, 128:]
    panel_inverse = jnp.stack(
        swap_halves(jnp.where(first, left, right), jnp.where(first, right, left))
    )

    shares = diagonal_partial(columns, panel_rows).reshape(8, 256, 128)
    shares = lax.all_to_all(shares, ("zh", "core"), split_axis=0, concat_axis=0, tiled=True)
    summed = jnp.sum(shares.reshape(4, 2, 256, 128).astype(jnp.float32), axis=0)
    diagonal_inverse = (pivot_inverse.astype(jnp.float32) - summed).astype(jnp.bfloat16)
    return (panel_inverse, diagonal_inverse)


def solution(mesh):
    fine = Mesh(mesh.devices.reshape(SIZES), AXES)
    row, col = ("zh", "y"), ("zl", "x", "core")
    in_specs = (P(row, col), P(None, row, col), P(), P(None, row, col))
    out_specs = (P(None, row, col), P(None, row, col))
    return jax.shard_map(
        on_device, mesh=fine, in_specs=in_specs, out_specs=out_specs, check_vma=False
    )
```

```python
import jax
import jax.numpy as jnp
from jax import lax
from jax.experimental import pallas as pl
from jax.experimental.pallas import tpu as pltpu
from jax.sharding import Mesh, PartitionSpec as P

SUPERNODES = 2
TILE = 128
AXES = ("zh", "y", "zl", "x", "core")
SIZES = (4, 4, 4, 4, 2)
CONTRACT_ROWS = (((0,), (0,)), ((), ()))
VMEM_BYTES = 60 * 1024 * 1024


def pairs(move):
    listed = []
    for zh in range(4):
        for y in range(4):
            for zl in range(4):
                for x in range(4):
                    for core in range(2):
                        place = []
                        for at in ((zh, y, zl, x, core), move(zh, y, zl, x, core)):
                            index = 0
                            for size, coordinate in zip(SIZES, at):
                                index = index * size + coordinate
                            place.append(index)
                        listed.append(tuple(place))
    return listed


SWAP_CORES = pairs(lambda zh, y, zl, x, core: (zh, y, zl, x, 1 - core))
TURN = pairs(lambda zh, y, zl, x, core: (zh, x, zl, y, core))
TURN_AND_SWAP = pairs(lambda zh, y, zl, x, core: (zh, x, zl, y, 1 - core))


def move(value, listed):
    return lax.ppermute(value, AXES, listed)


def panel_kernel(block_ref, rows_ref, out_ref):
    half = block_ref.shape[3]
    total = jnp.zeros(out_ref.shape[1:], jnp.float32)
    for group in range(4):
        for part in range(2):
            total += lax.dot_general(
                block_ref[0, part, group], rows_ref[group, part * half : part * half + half, :],
                CONTRACT_ROWS, preferred_element_type=jnp.float32,
            )
    out_ref[0] = total.astype(out_ref.dtype)


def panel_partial(block, rows):
    groups, parts, steps, half, height = block.shape
    width = rows.shape[2]
    return pl.pallas_call(
        panel_kernel,
        grid=(groups,),
        in_specs=[
            pl.BlockSpec((1, parts, steps, half, height), lambda g: (g, 0, 0, 0, 0)),
            pl.BlockSpec(rows.shape, lambda g: (0, 0, 0)),
        ],
        out_specs=pl.BlockSpec((1, height, width), lambda g: (g, 0, 0)),
        out_shape=jax.ShapeDtypeStruct((groups, height, width), jnp.bfloat16),
        compiler_params=pltpu.CompilerParams(vmem_limit_bytes=VMEM_BYTES),
        cost_estimate=pl.CostEstimate(
            flops=4 * groups * steps * half * height * width,
            bytes_accessed=7 * 1024 * 1024,
            transcendentals=0,
        ),
    )(block, rows)


def diagonal_kernel(left_ref, right_ref, out_ref):
    total = jnp.zeros((left_ref.shape[3], right_ref.shape[2]), jnp.float32)
    for y in range(4):
        total += lax.dot_general(
            left_ref[y, 0], right_ref[y], CONTRACT_ROWS, preferred_element_type=jnp.float32
        )
    out_ref[0] = total.astype(out_ref.dtype)


def diagonal_partial(left, right):
    groups, steps, depth, width = left.shape
    return pl.pallas_call(
        diagonal_kernel,
        grid=(steps,),
        in_specs=[
            pl.BlockSpec((groups, 1, depth, width), lambda g: (0, g, 0, 0)),
            pl.BlockSpec(right.shape, lambda g: (0, 0, 0)),
        ],
        out_specs=pl.BlockSpec((1, width, 256), lambda g: (g, 0, 0)),
        out_shape=jax.ShapeDtypeStruct((4, width, 256), jnp.bfloat16),
        compiler_params=pltpu.CompilerParams(vmem_limit_bytes=VMEM_BYTES),
        cost_estimate=pl.CostEstimate(
            flops=2 * groups * steps * depth * width * 256,
            bytes_accessed=5 * 1024 * 1024,
            transcendentals=0,
        ),
    )(left, right)


def mask_kernel(value_ref, flag_ref, out_ref):
    out_ref[...] = value_ref[...] * flag_ref[...]


def masked_rows(value, flag):
    return pl.pallas_call(
        mask_kernel,
        out_shape=jax.ShapeDtypeStruct(value.shape, value.dtype),
        compiler_params=pltpu.CompilerParams(vmem_limit_bytes=VMEM_BYTES),
        cost_estimate=pl.CostEstimate(flops=400 * 10**9, bytes_accessed=10**6, transcendentals=0),
    )(value, flag)


def on_device(inverse_block, panels, structure, pivot_inverse):
    zh, y, x = (lax.axis_index(name) for name in ("zh", "y", "x"))
    core = lax.axis_index("core")
    first = core == 0
    local_rows = panels.shape[1]
    tiles_here = local_rows // TILE

    def flags(group):
        start = (zh * 4 + group) * tiles_here
        here = lax.dynamic_slice(structure, (core, start), (1, tiles_here))
        return jnp.repeat(here[0], TILE)[:, None]

    def own_and_other(pair):
        return jnp.where(first, pair[0], pair[1]), jnp.where(first, pair[1], pair[0])

    mine, theirs = own_and_other(panels)
    wide = jnp.concatenate(own_and_other((mine, move(theirs, SWAP_CORES))), axis=1)
    turned = move(wide, TURN)
    wide = wide * flags(y).astype(jnp.bfloat16)

    block_parts = lax.all_gather(inverse_block.T, "zl")
    block = lax.all_gather(block_parts, ("y", "core")).reshape((4, 2) + block_parts.shape)
    wide, block_parts = lax.optimization_barrier((wide, block_parts))
    panel_parts = lax.all_gather(wide, "zl")
    turned, panel_parts = lax.optimization_barrier((turned, panel_parts))
    rows = lax.all_gather(masked_rows(turned, flags(x).astype(jnp.bfloat16)), "zh")
    columns = lax.all_gather(panel_parts, "y")

    partial = panel_partial(block, rows)
    parts = lax.all_to_all(partial, "x", split_axis=0, concat_axis=0, tiled=True)
    weight = flags(x).astype(jnp.float32)
    panel = (-(jnp.sum(parts.astype(jnp.float32), axis=0) * weight)).astype(jnp.bfloat16)
    panel_rows = lax.all_gather(panel, "x")
    mine, theirs = own_and_other((panel[:, :128], panel[:, 128:]))
    panel_inverse = jnp.stack(own_and_other((move(mine, TURN), move(theirs, TURN_AND_SWAP))))

    shares = diagonal_partial(columns, panel_rows)
    shares = lax.all_to_all(shares, "zh", split_axis=0, concat_axis=0, tiled=True)
    summed = jnp.sum(shares.astype(jnp.float32), axis=0).astype(jnp.bfloat16)
    mine, theirs = own_and_other((summed[:, :128], summed[:, 128:]))
    summed = jnp.stack(own_and_other((move(mine, TURN), move(theirs, TURN_AND_SWAP))))
    diagonal_inverse = (pivot_inverse.astype(jnp.float32) - summed.astype(jnp.float32)).astype(jnp.bfloat16)
    return (panel_inverse, diagonal_inverse)


def solution(mesh):
    fine = Mesh(mesh.devices.reshape(SIZES), AXES)
    row, col = ("zh", "y"), ("zl", "x", "core")
    in_specs = (P(row, col), P(None, row, col), P(), P(None, row, col))
    out_specs = (P(None, row, col), P(None, row, col))
    return jax.shard_map(
        on_device, mesh=fine, in_specs=in_specs, out_specs=out_specs, check_vma=False
    )
```

```python
import jax
import jax.numpy as jnp
from jax import lax
from jax.experimental import pallas as pl
from jax.experimental.pallas import tpu as pltpu
from jax.sharding import Mesh, PartitionSpec as P

SUPERNODES = 2
TILE = 128
AXES = ("zh", "y", "zl", "x", "core")
SIZES = (4, 4, 4, 4, 2)
CONTRACT_ROWS = (((0,), (0,)), ((), ()))
VMEM_BYTES = 60 * 1024 * 1024


def pairs(move):
    listed = []
    for zh in range(4):
        for y in range(4):
            for zl in range(4):
                for x in range(4):
                    for core in range(2):
                        place = []
                        for at in ((zh, y, zl, x, core), move(zh, y, zl, x, core)):
                            index = 0
                            for size, coordinate in zip(SIZES, at):
                                index = index * size + coordinate
                            place.append(index)
                        listed.append(tuple(place))
    return listed


PAIR = pairs(lambda zh, y, zl, x, core: (zh, y, zl ^ 1, x, core))
CROSS = pairs(lambda zh, y, zl, x, core: (zh, y, zl ^ 2, x, core))
TURN = pairs(lambda zh, y, zl, x, core: (zh, x, zl, y, core))
TURN_AND_PAIR = pairs(lambda zh, y, zl, x, core: (zh, x, zl ^ 1, y, core))


def move(value, listed):
    return lax.ppermute(value, AXES, listed)


def panel_kernel(block_ref, rows_ref, out_ref):
    half = block_ref.shape[3]
    total = jnp.zeros(out_ref.shape[1:], jnp.float32)
    for group in range(4):
        for part in range(2):
            total += lax.dot_general(
                block_ref[0, part, group], rows_ref[group, part * half : part * half + half, :],
                CONTRACT_ROWS, preferred_element_type=jnp.float32,
            )
    out_ref[0] = total.astype(out_ref.dtype)


def panel_partial(block, rows):
    groups, parts, steps, half, height = block.shape
    width = rows.shape[2]
    return pl.pallas_call(
        panel_kernel,
        grid=(groups,),
        in_specs=[
            pl.BlockSpec((1, parts, steps, half, height), lambda g: (g, 0, 0, 0, 0)),
            pl.BlockSpec(rows.shape, lambda g: (0, 0, 0)),
        ],
        out_specs=pl.BlockSpec((1, height, width), lambda g: (g, 0, 0)),
        out_shape=jax.ShapeDtypeStruct((groups, height, width), jnp.bfloat16),
        compiler_params=pltpu.CompilerParams(vmem_limit_bytes=VMEM_BYTES),
        cost_estimate=pl.CostEstimate(
            flops=4 * groups * steps * half * height * width,
            bytes_accessed=7 * 1024 * 1024,
            transcendentals=0,
        ),
    )(block, rows)


def diagonal_kernel(left_ref, right_ref, out_ref):
    total = jnp.zeros((256, 256), jnp.float32)
    for group in range(4):
        total += lax.dot_general(
            left_ref[group, 0, 0], right_ref[group], CONTRACT_ROWS, preferred_element_type=jnp.float32
        )
    value = total.astype(out_ref.dtype)
    out_ref[0, 0] = value[:128]
    out_ref[1, 0] = value[128:]


def diagonal_partial(left, right):
    groups, cores, couples, depth, width = left.shape
    return pl.pallas_call(
        diagonal_kernel,
        grid=(couples, cores),
        in_specs=[
            pl.BlockSpec((groups, 1, 1, depth, width), lambda p, c: (0, c, p, 0, 0)),
            pl.BlockSpec(right.shape, lambda p, c: (0, 0, 0)),
        ],
        out_specs=pl.BlockSpec((2, 1, 128, 256), lambda p, c: (p, c, 0, 0)),
        out_shape=jax.ShapeDtypeStruct((4, cores, 128, 256), jnp.bfloat16),
        compiler_params=pltpu.CompilerParams(vmem_limit_bytes=VMEM_BYTES),
        cost_estimate=pl.CostEstimate(
            flops=2 * groups * cores * couples * depth * width * 256,
            bytes_accessed=5 * 1024 * 1024,
            transcendentals=0,
        ),
    )(left, right)


def mask_kernel(value_ref, flag_ref, out_ref):
    out_ref[...] = value_ref[...] * flag_ref[...]


def masked_rows(value, flag):
    return pl.pallas_call(
        mask_kernel,
        out_shape=jax.ShapeDtypeStruct(value.shape, value.dtype),
        compiler_params=pltpu.CompilerParams(vmem_limit_bytes=VMEM_BYTES),
        cost_estimate=pl.CostEstimate(flops=400 * 10**9, bytes_accessed=10**6, transcendentals=0),
    )(value, flag)


def on_device(inverse_block, panels, structure, pivot_inverse):
    zh, y, zl, x = (lax.axis_index(name) for name in ("zh", "y", "zl", "x"))
    sup = lax.rem(zl, 2)
    local_rows = panels.shape[1]
    tiles_here = local_rows // TILE

    def flags(group):
        start = (zh * 4 + group) * tiles_here
        here = lax.dynamic_slice(structure, (sup, start), (1, tiles_here))
        return jnp.repeat(here[0], TILE)[:, None]

    def ordered(position, mine, theirs):
        first = position == 0
        return jnp.where(first, mine, theirs), jnp.where(first, theirs, mine)

    mine, theirs = ordered(sup, panels[0], panels[1])
    wide = jnp.concatenate(ordered(sup, mine, move(theirs, PAIR)), axis=1)
    turned = move(wide, TURN)
    wide = wide * flags(y).astype(jnp.bfloat16)

    block_parts = lax.all_gather(inverse_block.T, "zl")
    block = lax.all_gather(block_parts, ("y", "core")).reshape((4, 2) + block_parts.shape)
    panel_parts = jnp.stack(ordered(zl // 2, wide, move(wide, CROSS)))
    columns = lax.all_gather(panel_parts, ("y", "core")).reshape((4, 2) + panel_parts.shape)
    rows = lax.all_gather(masked_rows(turned, flags(x).astype(jnp.bfloat16)), "zh")

    partial = panel_partial(block, rows)
    parts = lax.all_to_all(partial, "x", split_axis=0, concat_axis=0, tiled=True)
    weight = flags(x).astype(jnp.float32)
    panel = (-(jnp.sum(parts.astype(jnp.float32), axis=0) * weight)).astype(jnp.bfloat16)
    panel_rows = lax.all_gather(panel, "x")
    mine, theirs = ordered(sup, panel[:, :128], panel[:, 128:])
    panel_inverse = jnp.stack(ordered(sup, move(mine, TURN), move(theirs, TURN_AND_PAIR)))

    shares = diagonal_partial(columns, panel_rows).reshape(4, 256, 256)
    shares = lax.all_to_all(shares, "zh", split_axis=0, concat_axis=0, tiled=True)
    summed = jnp.sum(shares.astype(jnp.float32), axis=0).astype(jnp.bfloat16)
    mine, theirs = ordered(sup, summed[:, :128], summed[:, 128:])
    summed = jnp.stack(ordered(sup, move(mine, TURN), move(theirs, TURN_AND_PAIR)))
    diagonal_inverse = (pivot_inverse.astype(jnp.float32) - summed.astype(jnp.float32)).astype(jnp.bfloat16)
    return (panel_inverse, diagonal_inverse)


def solution(mesh):
    fine = Mesh(mesh.devices.reshape(SIZES), AXES)
    row, col = ("zh", "y"), ("zl", "x", "core")
    in_specs = (P(row, col), P(None, row, col), P(), P(None, row, col))
    out_specs = (P(None, row, col), P(None, row, col))
    return jax.shard_map(
        on_device, mesh=fine, in_specs=in_specs, out_specs=out_specs, check_vma=False
    )
```

```python
import jax
import jax.numpy as jnp
from jax import lax
from jax.experimental import pallas as pl
from jax.experimental.pallas import tpu as pltpu
from jax.sharding import Mesh, PartitionSpec as P

SUPERNODES = 2
TILE = 128
AXES = ("zh", "y", "zl", "x", "core")
SIZES = (4, 4, 4, 4, 2)
CONTRACT_ROWS = (((0,), (0,)), ((), ()))
VMEM_BYTES = 60 * 1024 * 1024


def pairs(move):
    listed = []
    for zh in range(4):
        for y in range(4):
            for zl in range(4):
                for x in range(4):
                    for core in range(2):
                        place = []
                        for at in ((zh, y, zl, x, core), move(zh, y, zl, x, core)):
                            index = 0
                            for size, coordinate in zip(SIZES, at):
                                index = index * size + coordinate
                            place.append(index)
                        listed.append(tuple(place))
    return listed


PAIR = pairs(lambda zh, y, zl, x, core: (zh, y, zl ^ 1, x, core))
CROSS = pairs(lambda zh, y, zl, x, core: (zh, y, zl ^ 2, x, core))
TURN = pairs(lambda zh, y, zl, x, core: (zh, x, zl, y, core))
TURN_AND_PAIR = pairs(lambda zh, y, zl, x, core: (zh, x, zl ^ 1, y, core))


def move(value, listed):
    return lax.ppermute(value, AXES, listed)


def panel_partial(block, rows):
    rows = rows.reshape(rows.shape[0], 2, block.shape[3], rows.shape[2])
    partial = jnp.einsum("ycztS,zctj->ySj", block, rows, preferred_element_type=jnp.float32)
    return partial.astype(jnp.bfloat16)


def diagonal_partial(left, right):
    partial = jnp.einsum("gcpsi,gsj->pcij", left, right, preferred_element_type=jnp.float32)
    partial = partial.astype(jnp.bfloat16).reshape(2, 2, 2, 128, 256)
    return partial.transpose(0, 2, 1, 3, 4)


def mask_kernel(value_ref, flag_ref, out_ref):
    out_ref[...] = value_ref[...] * flag_ref[...]


def masked_rows(value, flag):
    return pl.pallas_call(
        mask_kernel,
        out_shape=jax.ShapeDtypeStruct(value.shape, value.dtype),
        compiler_params=pltpu.CompilerParams(vmem_limit_bytes=VMEM_BYTES),
        cost_estimate=pl.CostEstimate(flops=400 * 10**9, bytes_accessed=10**6, transcendentals=0),
    )(value, flag)


def on_device(inverse_block, panels, structure, pivot_inverse):
    zh, y, zl, x = (lax.axis_index(name) for name in ("zh", "y", "zl", "x"))
    sup = lax.rem(zl, 2)
    local_rows = panels.shape[1]
    tiles_here = local_rows // TILE

    def flags(group):
        start = (zh * 4 + group) * tiles_here
        here = lax.dynamic_slice(structure, (sup, start), (1, tiles_here))
        return jnp.repeat(here[0], TILE)[:, None]

    def ordered(position, mine, theirs):
        first = position == 0
        return jnp.where(first, mine, theirs), jnp.where(first, theirs, mine)

    mine, theirs = ordered(sup, panels[0], panels[1])
    wide = jnp.concatenate(ordered(sup, mine, move(theirs, PAIR)), axis=1)
    turned = move(wide, TURN)
    wide = wide * flags(y).astype(jnp.bfloat16)

    block_parts = lax.all_gather(inverse_block.T, "zl")
    block = lax.all_gather(block_parts, ("y", "core")).reshape((4, 2) + block_parts.shape)
    panel_parts = jnp.stack(ordered(zl // 2, wide, move(wide, CROSS)))
    columns = lax.all_gather(panel_parts, ("y", "core")).reshape((4, 2) + panel_parts.shape)
    rows = lax.all_gather(masked_rows(turned, flags(x).astype(jnp.bfloat16)), "zh")

    partial = panel_partial(block, rows)
    parts = lax.all_to_all(partial, "x", split_axis=0, concat_axis=0, tiled=True)
    weight = flags(x).astype(jnp.float32)
    panel = (-(jnp.sum(parts.astype(jnp.float32), axis=0) * weight)).astype(jnp.bfloat16)
    panel_rows = lax.all_gather(panel, "x")
    mine, theirs = ordered(sup, panel[:, :128], panel[:, 128:])
    panel_inverse = jnp.stack(ordered(sup, move(mine, TURN), move(theirs, TURN_AND_PAIR)))

    shares = diagonal_partial(columns, panel_rows).reshape(4, 256, 256)
    shares = lax.all_to_all(shares, "zh", split_axis=0, concat_axis=0, tiled=True)
    summed = jnp.sum(shares.astype(jnp.float32), axis=0).astype(jnp.bfloat16)
    mine, theirs = ordered(sup, summed[:, :128], summed[:, 128:])
    summed = jnp.stack(ordered(sup, move(mine, TURN), move(theirs, TURN_AND_PAIR)))
    diagonal_inverse = (pivot_inverse.astype(jnp.float32) - summed.astype(jnp.float32)).astype(jnp.bfloat16)
    return (panel_inverse, diagonal_inverse)


def solution(mesh):
    fine = Mesh(mesh.devices.reshape(SIZES), AXES)
    row, col = ("zh", "y"), ("zl", "x", "core")
    in_specs = (P(row, col), P(None, row, col), P(), P(None, row, col))
    out_specs = (P(None, row, col), P(None, row, col))
    return jax.shard_map(
        on_device, mesh=fine, in_specs=in_specs, out_specs=out_specs, check_vma=False
    )
```

```python
import jax
import jax.numpy as jnp
from jax import lax
from jax.sharding import Mesh, PartitionSpec as P

SUPERNODES = 2
TILE = 128
AXES = ("zh", "y", "zl", "x", "core")
SIZES = (4, 4, 4, 4, 2)


def pairs(move):
    listed = []
    for zh in range(4):
        for y in range(4):
            for zl in range(4):
                for x in range(4):
                    for core in range(2):
                        place = []
                        for at in ((zh, y, zl, x, core), move(zh, y, zl, x, core)):
                            index = 0
                            for size, coordinate in zip(SIZES, at):
                                index = index * size + coordinate
                            place.append(index)
                        listed.append(tuple(place))
    return listed


BOTH_WAYS = [[0, 2, 4, 6], [7, 5, 3, 1]]
PAIR = pairs(lambda zh, y, zl, x, core: (zh, y, zl ^ 1, x, core))
CROSS = pairs(lambda zh, y, zl, x, core: (zh, y, zl ^ 2, x, core))
TURN = pairs(lambda zh, y, zl, x, core: (zh, x, zl, y, core))
TURN_AND_PAIR = pairs(lambda zh, y, zl, x, core: (zh, x, zl ^ 1, y, core))


def move(value, listed):
    return lax.ppermute(value, AXES, listed)


def panel_partial(block, rows):
    rows = rows.reshape(rows.shape[0], 2, block.shape[3], rows.shape[2])
    partial = jnp.einsum("ycztS,zctj->ySj", block, rows, preferred_element_type=jnp.float32)
    return partial.astype(jnp.bfloat16)


def diagonal_partial(left, right):
    partial = jnp.einsum("gcpsi,gsj->pcij", left, right, preferred_element_type=jnp.float32)
    partial = partial.astype(jnp.bfloat16).reshape(2, 2, 2, 128, 256)
    return partial.transpose(0, 2, 1, 3, 4)


def on_device(inverse_block, panels, structure, pivot_inverse):
    zh, y, zl, x = (lax.axis_index(name) for name in ("zh", "y", "zl", "x"))
    sup = lax.rem(zl, 2)
    local_rows = panels.shape[1]
    tiles_here = local_rows // TILE

    def flags(group):
        start = (zh * 4 + group) * tiles_here
        here = lax.dynamic_slice(structure, (sup, start), (1, tiles_here))
        return jnp.repeat(here[0], TILE)[:, None]

    def ordered(position, mine, theirs):
        first = position == 0
        return jnp.where(first, mine, theirs), jnp.where(first, theirs, mine)

    mine, theirs = ordered(sup, panels[0], panels[1])
    block_parts = lax.all_gather(inverse_block.T, "zl")
    theirs, block_parts = lax.optimization_barrier((move(theirs, PAIR), block_parts))
    wide = jnp.concatenate(ordered(sup, mine, theirs), axis=1)
    wide = wide * flags(y).astype(jnp.bfloat16)
    turned = move(wide, TURN)

    block = lax.all_gather(block_parts, ("y", "core")).reshape((4, 2) + block_parts.shape)
    panel_parts = jnp.stack(ordered(zl // 2, wide, move(wide, CROSS)))
    turned, panel_parts = lax.optimization_barrier((turned, panel_parts))
    columns = lax.all_gather(panel_parts, ("y", "core")).reshape((4, 2) + panel_parts.shape)
    rows = lax.all_gather(turned, "zh")

    partial = panel_partial(block, rows)
    parts = lax.all_to_all(partial, "x", split_axis=0, concat_axis=0, tiled=True)
    weight = flags(x).astype(jnp.float32)
    panel = (-(jnp.sum(parts.astype(jnp.float32), axis=0) * weight)).astype(jnp.bfloat16)
    panel_rows = lax.all_gather(panel, "x")
    mine, theirs = ordered(sup, panel[:, :128], panel[:, 128:])
    panel_moved = move(mine, TURN), move(theirs, TURN_AND_PAIR)

    shares = diagonal_partial(columns, panel_rows).reshape(4, 256, 256)
    shares = jnp.where(lax.axis_index("core") == 0, shares, shares[::-1])
    shares = lax.all_to_all(
        shares, ("zh", "core"), split_axis=0, concat_axis=0, tiled=True, axis_index_groups=BOTH_WAYS
    )
    summed = jnp.sum(shares.astype(jnp.float32), axis=0).astype(jnp.bfloat16)
    mine, theirs = ordered(sup, summed[:, :128], summed[:, 128:])
    summed = move(mine, TURN), move(theirs, TURN_AND_PAIR)
    panel_inverse = jnp.stack(ordered(sup, *panel_moved))
    summed = jnp.stack(ordered(sup, *summed))
    diagonal_inverse = (pivot_inverse.astype(jnp.float32) - summed.astype(jnp.float32)).astype(jnp.bfloat16)
    return (panel_inverse, diagonal_inverse)


def solution(mesh):
    fine = Mesh(mesh.devices.reshape(SIZES), AXES)
    row, col = ("zh", "y"), ("zl", "x", "core")
    in_specs = (P(row, col), P(None, row, col), P(), P(None, row, col))
    out_specs = (P(None, row, col), P(None, row, col))
    return jax.shard_map(
        on_device, mesh=fine, in_specs=in_specs, out_specs=out_specs, check_vma=False
    )
```

```python
import jax
import jax.numpy as jnp
from jax import lax
from jax.sharding import Mesh, PartitionSpec as P

SUPERNODES = 2
TILE = 128
AXES = ("zh", "y", "zl", "x", "core")
SIZES = (4, 4, 4, 4, 2)


def pairs(move):
    listed = []
    for zh in range(4):
        for y in range(4):
            for zl in range(4):
                for x in range(4):
                    for core in range(2):
                        place = []
                        for at in ((zh, y, zl, x, core), move(zh, y, zl, x, core)):
                            index = 0
                            for size, coordinate in zip(SIZES, at):
                                index = index * size + coordinate
                            place.append(index)
                        listed.append(tuple(place))
    return listed


BOTH_WAYS = [[0, 2, 4, 6], [7, 5, 3, 1]]
PAIR = pairs(lambda zh, y, zl, x, core: (zh, y, zl ^ 1, x, core))
CROSS = pairs(lambda zh, y, zl, x, core: (zh, y, zl ^ 2, x, core))
TURN = pairs(lambda zh, y, zl, x, core: (zh, x, zl, y, core))
TURN_AND_PAIR = pairs(lambda zh, y, zl, x, core: (zh, x, zl ^ 1, y, core))


def move(value, listed):
    return lax.ppermute(value, AXES, listed)


def panel_partial(block, rows):
    rows = rows.reshape(rows.shape[0], 2, block.shape[3], rows.shape[2])
    partial = jnp.einsum("ycztS,zctj->ySj", block, rows, preferred_element_type=jnp.float32)
    return partial.astype(jnp.bfloat16)


def diagonal_partial(left, right):
    partial = jnp.einsum("gcpsi,gsj->pcij", left, right, preferred_element_type=jnp.float32)
    partial = partial.astype(jnp.bfloat16).reshape(2, 2, 2, 128, 256)
    return partial.transpose(0, 2, 1, 3, 4)


def on_device(inverse_block, panels, structure, pivot_inverse):
    zh, y, zl, x = (lax.axis_index(name) for name in ("zh", "y", "zl", "x"))
    sup = lax.rem(zl, 2)
    local_rows = panels.shape[1]
    tiles_here = local_rows // TILE

    def flags(group):
        start = (zh * 4 + group) * tiles_here
        here = lax.dynamic_slice(structure, (sup, start), (1, tiles_here))
        return jnp.repeat(here[0], TILE)[:, None]

    def ordered(position, mine, theirs):
        first = position == 0
        return jnp.where(first, mine, theirs), jnp.where(first, theirs, mine)

    mine, theirs = ordered(sup, panels[0], panels[1])
    block_parts = lax.all_gather(inverse_block.T, "zl")
    theirs, block_parts = lax.optimization_barrier((move(theirs, PAIR), block_parts))
    wide = jnp.concatenate(ordered(sup, mine, theirs), axis=1)
    wide = wide * flags(y).astype(jnp.bfloat16)
    turned = move(wide, TURN)

    block = lax.all_gather(block_parts, ("y", "core")).reshape((4, 2) + block_parts.shape)
    panel_parts = jnp.stack(ordered(zl // 2, wide, move(wide, CROSS)))
    turned, panel_parts = lax.optimization_barrier((turned, panel_parts))
    columns = lax.all_gather(panel_parts, ("y", "core")).reshape((4, 2) + panel_parts.shape)
    rows = lax.all_gather(turned, "zh")

    partial = panel_partial(block, rows)
    partial = jnp.where(lax.axis_index("core") == 0, partial, partial[::-1])
    parts = lax.all_to_all(
        partial, ("x", "core"), split_axis=0, concat_axis=0, tiled=True, axis_index_groups=BOTH_WAYS
    )
    weight = flags(x).astype(jnp.float32)
    panel = (-(jnp.sum(parts.astype(jnp.float32), axis=0) * weight)).astype(jnp.bfloat16)
    panel_rows = lax.all_gather(panel, "x")
    mine, theirs = ordered(sup, panel[:, :128], panel[:, 128:])
    panel_moved = move(mine, TURN), move(theirs, TURN_AND_PAIR)

    shares = diagonal_partial(columns, panel_rows).reshape(4, 256, 256)
    shares = jnp.where(lax.axis_index("core") == 0, shares, shares[::-1])
    shares = lax.all_to_all(
        shares, ("zh", "core"), split_axis=0, concat_axis=0, tiled=True, axis_index_groups=BOTH_WAYS
    )
    summed = jnp.sum(shares.astype(jnp.float32), axis=0).astype(jnp.bfloat16)
    mine, theirs = ordered(sup, summed[:, :128], summed[:, 128:])
    summed = move(mine, TURN), move(theirs, TURN_AND_PAIR)
    panel_inverse = jnp.stack(ordered(sup, *panel_moved))
    summed = jnp.stack(ordered(sup, *summed))
    diagonal_inverse = (pivot_inverse.astype(jnp.float32) - summed.astype(jnp.float32)).astype(jnp.bfloat16)
    return (panel_inverse, diagonal_inverse)


def solution(mesh):
    fine = Mesh(mesh.devices.reshape(SIZES), AXES)
    row, col = ("zh", "y"), ("zl", "x", "core")
    in_specs = (P(row, col), P(None, row, col), P(), P(None, row, col))
    out_specs = (P(None, row, col), P(None, row, col))
    return jax.shard_map(
        on_device, mesh=fine, in_specs=in_specs, out_specs=out_specs, check_vma=False
    )
```
